32 devices in a mesh: site: 8 (over y, x, core), real: 4 (over z).
Axes of the slice: x: 2, y: 2, z: 4, core: 2. Of those that a mesh axis runs over, the one named last changes fastest.
Arguments:
- field: float32 [64, 16384], P('real', 'site'), may hold values from -6 to 6
- observed: float32 [20480], P('site'), may hold values from -6 to 6
- inv_cov: float32 [20480, 20480], P('site', 'real'), may hold values from -0.0012207031 to 0.0012207031
- site_xy: float32 [2, 16384], P(None, 'site'), may hold values from 0 to 200
- station_site: int32 [20480], P('site'), may hold values from 0 to 16383, as said below
- site_mean: float32 [16384], P('site'), may hold values from -3 to 0
- building_site: int32 [32768], P('site'), may hold values from 0 to 16383, as said below
- building_class: int32 [32768], P('site'), may hold values from 0 to 35
- building_tract: int32 [32768], P('site'), may hold values from 0 to 4095
- building_value: float32 [32768], P('site')
- median_ln: float32 [4, 36], replicated, may hold values from -2.3 to 0.4
- beta_ln: float32 [36], replicated, may hold values from 0.4 to 0.8
- loss_step: float32 [4, 36], replicated, may hold values from 0.02 to 0.3
Outputs:
- cond_field: float32 [64, 16384], P('real', 'site')
- tract_loss: float32 [64, 4096], P('real', 'site')
- total_loss: float32 [64], P('real')
The draws below stay inside these ranges and needn't reach their ends.
Inputs may be any that keep to these rules, and one draw needn't show every extreme that they name: `station_site`: the stations of rows d * 2560 to (d + 1) * 2560 - 1 stand at sites d * 2048 to (d + 1) * 2048 - 1; several stations may share a site. `building_site`: the buildings of rows d * 4096 to (d + 1) * 4096 - 1 stand at sites d * 2048 to (d + 1) * 2048 - 1.
All inputs are finite; a program needn't handle non-finite values.
Results may differ from the reference program's by a relative error of at most 0.003.
Values may be sent and summed in bfloat16 or wider, within the bound.
A program may use at most 128 MiB of HBM per device.

```python
import math
import jax
import jax.numpy as jnp
from jax import lax

R = 64
NS = 20480
NCLASS = 36
DS = 4
SITE_DEV = 2048
NS_DEV = 2560
NSITE = 16384
BLD_DEV = 4096
NB = 32768
NTRACT = 4096


def draw_station_site(key, part):
    own_key = jax.random.fold_in(key, 7331)
    rows = jnp.arange(NS, dtype=jnp.int32)
    base = rows // NS_DEV * SITE_DEV
    return (base + jax.random.randint(own_key, (NS,), 0, SITE_DEV, dtype=jnp.int32)).astype(jnp.int32)


def draw_building_site(key, part):
    own_key = jax.random.fold_in(key, 9173)
    rows = jnp.arange(NB, dtype=jnp.int32)
    base = rows // BLD_DEV * SITE_DEV
    return (base + jax.random.randint(own_key, (NB,), 0, SITE_DEV, dtype=jnp.int32)).astype(jnp.int32)


def draw_building_value(key, part):
    rows = jnp.arange(NB, dtype=jnp.int32).astype(jnp.float32)
    trend = 1.0 + 2.0 * rows / (NB - 1)
    spread = jnp.exp(jax.random.uniform(key, (NB,), jnp.float32, jnp.log(0.3), jnp.log(3.0)))
    return (0.5 * trend * spread).astype(jnp.float32)


def with_ends(array, key, smallest, top_value):
    dims = array.shape
    place = [jax.random.randint(jax.random.fold_in(key, axis), (), 0, dims[axis]) for axis in range(len(dims))]
    array = array.at[tuple(place)].set(smallest)
    longest = dims.index(max(dims))
    place[longest] = (place[longest] + 1) % dims[longest]
    return array.at[tuple(place)].set(top_value)


def levels(key, dims, cuts, smallest, largest):
    loudness = 1.0
    for axis_at, blocks in cuts:
        steps = jax.random.uniform(jax.random.fold_in(jax.random.fold_in(key, 6), axis_at), (blocks,), jnp.float32, smallest / len(cuts), largest / len(cuts))
        loudness = loudness * jnp.repeat(jnp.exp(steps), dims[axis_at] // blocks).reshape((-1,) + (1,) * (len(dims) - 1 - axis_at))
    return loudness


def scatter_about(rng, extent, scale, most, cuts=(), held_as=jnp.bfloat16):
    result = jax.random.normal(rng, extent, jnp.float32) * scale
    if len(cuts) > 0:
        result = levels(rng, extent, cuts, -0.22, 0.18) * result
    return jnp.clip(result, min=-most, max=most).astype(held_as)


def setup_inputs(seed: int = 0) -> dict:
    splits = jax.random.split(jax.random.key(seed), 14)
    field = scatter_about(splits[0], (R, NSITE), 1.0, 6.0, ((0, 4), (1, 8)), jnp.float32)
    observed = scatter_about(splits[1], (NS,), 1.0, 6.0, ((0, 8),), jnp.float32)
    inv_cov = scatter_about(splits[2], (NS, NS), (NS * NS // 16) ** -0.5, 0.0012207031, ((0, 8), (1, 4)), jnp.float32)
    site_xy = jnp.clip(200.0 * jax.random.uniform(splits[3], (2, NSITE), jnp.float32) ** levels(splits[3], (2, NSITE), ((1, 8),), -0.2, 0.2), 0.0, 200.0)
    station_site = draw_station_site(jax.random.fold_in(splits[13], 71), 0)
    site_mean = jnp.clip(-3.0 + 3.0 * jax.random.uniform(splits[5], (NSITE,), jnp.float32) ** levels(splits[5], (NSITE,), ((0, 8),), -0.2, 0.2), -3.0, 0.0)
    building_site = draw_building_site(jax.random.fold_in(splits[13], 71), 0)
    building_class = with_ends(jax.random.randint(splits[7], (NB,), 0, NCLASS), jax.random.fold_in(splits[7], 1), 0, NCLASS - 1).astype(jnp.int32)
    building_tract = with_ends(jax.random.randint(splits[8], (NB,), 0, NTRACT), jax.random.fold_in(splits[8], 1), 0, NTRACT - 1).astype(jnp.int32)
    building_value = draw_building_value(jax.random.fold_in(splits[13], 71), 0)
    median_ln = jnp.clip(jax.random.uniform(splits[10], (DS, NCLASS), jnp.float32, -2.3, 0.4), -2.3, 0.4)
    beta_ln = jnp.clip(jax.random.uniform(splits[11], (NCLASS,), jnp.float32, 0.4, 0.8), 0.4, 0.8)
    loss_step = jnp.clip(jax.random.uniform(splits[12], (DS, NCLASS), jnp.float32, 0.02, 0.3), 0.02, 0.3)
    return dict(field=field, observed=observed, inv_cov=inv_cov, site_xy=site_xy, station_site=station_site, site_mean=site_mean, building_site=building_site, building_class=building_class, building_tract=building_tract, building_value=building_value, median_ln=median_ln, beta_ln=beta_ln, loss_step=loss_step)


def normal_cdf(value):
    return 0.5 * (1.0 + lax.erf(value * 0.7071067811865476))

def reference(field, observed, inv_cov, site_xy, station_site, site_mean, building_site, building_class, building_tract, building_value, median_ln, beta_ln, loss_step):
    station_field = jnp.take(field, station_site, axis=1)
    innov = observed[None, :] - station_field
    weights = jnp.dot(innov, inv_cov, precision=lax.Precision.HIGHEST, preferred_element_type=jnp.float32).astype(jnp.bfloat16)
    station_xy = jnp.take(site_xy, station_site, axis=1)
    width = math.gcd(NSITE, 1024)
    count = NSITE // width

    def one_block(index):
        anchor = (index * width).astype(jnp.int32)
        east = lax.dynamic_slice_in_dim(site_xy[0], anchor, width)
        north = lax.dynamic_slice_in_dim(site_xy[1], anchor, width)
        dist = jnp.sqrt((east[:, None] - station_xy[0][None, :]) ** 2 + (north[:, None] - station_xy[1][None, :]) ** 2)
        cross = jnp.exp(-dist / 30.0).astype(jnp.bfloat16)
        return lax.dot_general(weights, cross, (((1,), (1,)), ((), ())), preferred_element_type=jnp.float32)
    pieces = lax.map(one_block, jnp.arange(count, dtype=jnp.int32))
    cond_field = field + pieces.transpose(1, 0, 2).reshape(R, NSITE)
    ln_im = site_mean[None, :] + 0.6 * cond_field
    build_im = jnp.take(ln_im, building_site, axis=1)
    median_b = median_ln[:, building_class]
    beta_b = beta_ln[building_class]
    step_b = loss_step[:, building_class]
    exceed = normal_cdf((build_im[None, :, :] - median_b[:, None, :]) / beta_b[None, None, :])
    loss = building_value[None, :] * lax.optimization_barrier(jnp.sum(exceed * step_b[:, None, :], axis=0))
    tract_loss = jax.ops.segment_sum(loss.T, building_tract, NTRACT).T
    total_loss = lax.optimization_barrier(jnp.sum(loss, axis=1)) / NB
    return (cond_field, tract_loss, total_loss)
```

```python
import functools
import math

import jax
import jax.numpy as jnp
from jax import lax
from jax.experimental import pallas as pl
from jax.experimental.pallas import tpu as pltpu
from jax.sharding import PartitionSpec as P

MESH = pl.DeviceIdType.MESH
F32 = jnp.float32
BF16 = jnp.bfloat16
COORD_SCALE = math.log2(math.e) / 30.0
TRACT_DEV = 512


def split2(x):
    hi = x.astype(BF16).astype(F32)
    return hi, x - hi


def split3(x):
    hi, rest = split2(x)
    mid, low = split2(rest)
    return hi, mid, low


def onehot_gather(table_ref, index_ref, width, block, store):
    count = index_ref.shape[1]
    sites = table_ref.shape[1]

    def chunk(n, carry):
        start = pl.multiple_of(n * width, 128)
        index = index_ref[:, pl.ds(start, width)]
        total = jnp.zeros((table_ref.shape[0], width), F32)
        for s in range(sites // block):
            rows = lax.broadcasted_iota(jnp.int32, (block, width), 0) + s * block
            hot = jnp.where(rows == index, 1.0, 0.0).astype(BF16)
            total += jnp.dot(
                table_ref[:, s * block : (s + 1) * block], hot, preferred_element_type=F32
            )
        store(start, total)
        return carry

    lax.fori_loop(0, count // width, chunk, 0)


def krige_kernel(
    n_site,
    n_real,
    groups,
    steps,
    nbuf,
    field_ref,
    observed_ref,
    inv_ref,
    xy_ref,
    local_ref,
    cond_ref,
    table,
    innov_all,
    xy_rows,
    xy_col,
    tiles,
    cross,
    part,
    got,
    wout,
    acc,
    back,
    back_in,
    tile_sem,
    i_send,
    i_recv,
    x_send,
    x_recv,
    p_send,
    p_recv,
    w_send,
    w_recv,
    b_send,
    b_recv,
):
    me_s = lax.axis_index("site")
    me_r = lax.axis_index("real")
    rr, sites = field_ref.shape
    ns = observed_ref.shape[1]
    reals = n_real * rr
    per = n_site // n_real
    tw = tiles.shape[2]
    gw = tw * steps
    rows_o = reals // n_site
    k = 16 // rows_o
    mw = gw // k
    total_steps = groups * steps

    barrier = pltpu.get_barrier_semaphore()
    for j in range(1, n_site):
        pl.semaphore_signal(
            barrier, inc=1, device_id=(lax.rem(me_s + j, n_site), me_r), device_id_type=MESH
        )
    for j in range(1, n_real):
        pl.semaphore_signal(
            barrier, inc=1, device_id=(me_s, lax.rem(me_r + j, n_real)), device_id_type=MESH
        )

    def tile_copy(c):
        slot = lax.rem(c, nbuf)
        col = pl.multiple_of(c * tw, 128)
        return pltpu.make_async_copy(
            inv_ref.at[:, pl.ds(col, tw)], tiles.at[slot], tile_sem.at[slot]
        )

    for c in range(nbuf):
        tile_copy(c).start()

    fh, fl = split2(field_ref[...])
    xa, xb, xc = split3(xy_ref[...] * COORD_SCALE)
    table[...] = jnp.concatenate(
        [fh, fl, xa, xb, xc, jnp.zeros((10, sites), F32)], axis=0
    ).astype(BF16)

    me_slot = lax.rem(me_s, per)
    mine = me_s // per == me_r

    def store(start, got_rows):
        width = got_rows.shape[1]
        station = got_rows[:rr] + got_rows[rr : 2 * rr]
        xys = (
            got_rows[2 * rr : 2 * rr + 2]
            + got_rows[2 * rr + 2 : 2 * rr + 4]
            + got_rows[2 * rr + 4 : 2 * rr + 6]
        )
        innov = observed_ref[:, pl.ds(start, width)] - station
        hi, low = split2(innov)
        innov_all[me_r, :, pl.ds(start, width)] = jnp.concatenate([hi, low], axis=0).astype(BF16)
        xy_rows[per, :, pl.ds(start, width)] = jnp.concatenate(
            [xys, jnp.zeros((6, width), F32)], axis=0
        )

    onehot_gather(table, local_ref, math.gcd(ns, 512), 256, store)

    pl.semaphore_wait(barrier, n_site - 1 + n_real - 1)

    def innov_copy(j):
        return pltpu.make_async_remote_copy(
            src_ref=innov_all.at[me_r],
            dst_ref=innov_all.at[me_r],
            send_sem=i_send.at[j],
            recv_sem=i_recv.at[j],
            device_id=(me_s, lax.rem(me_r + j, n_real)),
            device_id_type=MESH,
        )

    def xy_copy(j):
        return pltpu.make_async_remote_copy(
            src_ref=xy_rows.at[per],
            dst_ref=xy_rows.at[me_slot],
            send_sem=x_send.at[j],
            recv_sem=x_recv.at[me_slot],
            device_id=(lax.rem(me_s + j, n_site), me_r),
            device_id_type=MESH,
        )

    @pl.when(mine)
    def _():
        for j in range(1, n_site):
            xy_copy(j).start()

    for j in range(1, n_real):
        innov_copy(j).start()

    @pl.when(mine)
    def _():
        xy_rows[me_slot] = xy_rows[per]

    for s in range(per):

        @pl.when(jnp.logical_not(jnp.logical_and(mine, me_slot == s)))
        def _():
            pltpu.make_async_remote_copy(
                src_ref=xy_rows.at[per],
                dst_ref=xy_rows.at[s],
                send_sem=x_send.at[0],
                recv_sem=x_recv.at[s],
                device_id=(lax.rem(me_s + 1, n_site), me_r),
                device_id_type=MESH,
            ).wait_recv()

    for s in range(per):
        xy_col[s * ns : (s + 1) * ns, :] = xy_rows[s].T

    for j in range(1, n_real):
        innov_copy(j).wait_recv()

    east = xy_ref[0:1, :] * COORD_SCALE
    north = xy_ref[1:2, :] * COORD_SCALE
    kt = math.gcd(ns, 256)
    k_count = ns // kt
    pieces = tw // 16
    acc[...] = jnp.zeros_like(acc)

    def part_copy(g, j):
        peer = lax.rem(me_s + j, n_site)
        return pltpu.make_async_remote_copy(
            src_ref=part.at[g, peer],
            dst_ref=got.at[g, me_s],
            send_sem=p_send.at[g, j],
            recv_sem=p_recv.at[g, j],
            device_id=(peer, me_r),
            device_id_type=MESH,
        )

    def w_copy(g, j):
        peer = lax.rem(me_s + j, n_site)
        return pltpu.make_async_remote_copy(
            src_ref=wout.at[g, me_s],
            dst_ref=wout.at[g, me_s],
            send_sem=w_send.at[g, j],
            recv_sem=w_recv.at[g, j],
            device_id=(peer, me_r),
            device_id_type=MESH,
        )

    def sum_and_share(g):
        for j in range(1, n_site):
            part_copy(g, j).wait_recv()
        got[g, me_s] = part[g, me_s]
        total = got[g, 0]
        for s in range(1, n_site):
            total += got[g, s]
        wout[g, me_s] = jnp.concatenate(
            [total[:, i * mw : (i + 1) * mw] for i in range(k)], axis=0
        ).astype(BF16)
        for j in range(1, n_site):
            w_copy(g, j).start()

    def apply_group(g, width, after):
        for j in range(1, n_site):
            w_copy(g, j).wait_recv()
        weights = wout[g].astype(F32)
        weights = jnp.concatenate(
            [
                jnp.concatenate(
                    [weights[s, i * rows_o : (i + 1) * rows_o] for i in range(k)], axis=1
                )
                for s in range(n_site)
            ],
            axis=0,
        ).astype(BF16)
        row = pl.multiple_of(g * gw, 128)
        for n in range(sites // width):
            cols = slice(n * width, (n + 1) * width)
            acc[:, cols] += jnp.dot(
                weights, cross[pl.ds(row, gw), cols], preferred_element_type=F32
            )
            after(n)

    def one_step(q, g):
        c = g * steps + q
        slot = lax.rem(c, nbuf)
        tile_copy(c).wait()
        lhs = innov_all[...].reshape(n_real * 2 * rr, ns)
        product = jnp.zeros((n_real * 2 * rr, tw), F32)
        done = 0
        for p in range(k_count):
            product += jnp.dot(
                lhs[:, p * kt : (p + 1) * kt],
                tiles[slot, p * kt : (p + 1) * kt, :].astype(BF16),
                preferred_element_type=F32,
            )
            upto = (p + 1) * pieces // k_count
            for m in range(done, upto):
                row = pl.multiple_of(c * tw + m * 16, 16)
                dx = xy_col[pl.ds(row, 16), 0:1] - east
                dy = xy_col[pl.ds(row, 16), 1:2] - north
                d2 = jnp.maximum(dx * dx + dy * dy, 1e-20)
                cross[pl.ds(row, 16), :] = jnp.exp2(-(d2 * lax.rsqrt(d2))).astype(BF16)
            done = upto
        product = product.reshape(n_real, 2, rr, tw)
        partial = (product[:, 0] + product[:, 1]).reshape(n_site, rows_o, tw)
        part[g, :, :, pl.ds(pl.multiple_of(q * tw, 128), tw)] = partial

        @pl.when(c + nbuf < total_steps)
        def _():
            tile_copy(c + nbuf).start()

        return g

    def one_group(g, carry):
        lax.fori_loop(0, steps, one_step, g)
        for j in range(1, n_site):
            part_copy(g, j).start()

        @pl.when(g >= 1)
        def _():
            sum_and_share(g - 1)

        @pl.when(g >= 2)
        def _():
            apply_group(g - 2, 512, lambda n: None)

        return carry

    lax.fori_loop(0, groups, one_group, 0)

    def back_copy(j, n):
        peer = lax.rem(me_r + j, n_real)
        return pltpu.make_async_remote_copy(
            src_ref=back.at[n, peer],
            dst_ref=back_in.at[n, me_r],
            send_sem=b_send.at[n, j],
            recv_sem=b_recv.at[n, j],
            device_id=(me_s, peer),
            device_id_type=MESH,
        )

    bw = back.shape[3] * (back.shape[2] // rr)
    kb = bw // back.shape[3]

    def send_back(n):
        for z in range(n_real):
            block = acc[z * rr : (z + 1) * rr, n * bw : (n + 1) * bw]
            w = bw // kb
            back[n, z] = jnp.concatenate(
                [block[:, i * w : (i + 1) * w] for i in range(kb)], axis=0
            ).astype(BF16)
        for j in range(1, n_real):
            back_copy(j, n).start()

    apply_group(groups - 2, 512, lambda n: None)
    sum_and_share(groups - 1)
    apply_group(groups - 1, bw, send_back)

    own_row = pl.multiple_of(me_r * rr, 8)
    for n in range(sites // bw):
        for j in range(1, n_real):
            back_copy(j, n).wait_recv()
        back_in[n, me_r] = jnp.zeros_like(back_in[n, 0])
        total = back_in[n, 0].astype(F32)
        for z in range(1, n_real):
            total += back_in[n, z].astype(F32)
        total = jnp.concatenate([total[i * rr : (i + 1) * rr] for i in range(kb)], axis=1)
        cols = slice(n * bw, (n + 1) * bw)
        cond_ref[:, cols] = field_ref[:, cols] + acc[pl.ds(own_row, rr), cols] + total

    for j in range(1, n_real):
        innov_copy(j).wait_send()
        for n in range(sites // bw):
            back_copy(j, n).wait_send()

    @pl.when(mine)
    def _():
        for j in range(1, n_site):
            xy_copy(j).wait_send()

    def drain(g, carry):
        for j in range(1, n_site):
            part_copy(g, j).wait_send()
            w_copy(g, j).wait_send()
        return carry

    lax.fori_loop(0, groups, drain, 0)


def loss_kernel(
    n_site,
    all_buildings,
    cond_ref,
    mean_ref,
    local_ref,
    class_ref,
    tract_ref,
    value_ref,
    params_ref,
    out_ref,
    sum_ref,
    table,
    loss_ref,
    lo_hot,
    send,
    recv,
    s_sem,
    r_sem,
):
    me_s = lax.axis_index("site")
    me_r = lax.axis_index("real")
    rr = cond_ref.shape[0]
    count = local_ref.shape[1]
    barrier = pltpu.get_barrier_semaphore()
    for j in range(1, n_site):
        pl.semaphore_signal(
            barrier, inc=1, device_id=(lax.rem(me_s + j, n_site), me_r), device_id_type=MESH
        )
    hi, low = split2(mean_ref[...] + 0.6 * cond_ref[...])
    table[...] = jnp.concatenate([hi, low], axis=0).astype(BF16)
    classes = params_ref.shape[1]

    def store(start, rows):
        width = rows.shape[1]
        here = pl.ds(start, width)
        im = rows[:rr] + rows[rr:]
        hot = jnp.where(
            lax.broadcasted_iota(jnp.int32, (classes, width), 0) == class_ref[:, here], 1.0, 0.0
        )
        par = jnp.dot(
            params_ref[...], hot, precision=lax.Precision.HIGHEST, preferred_element_type=F32
        )
        inverse = 0.7071067811865476 / par[4:5]
        total = jnp.zeros((rr, width), F32)
        for s in range(4):
            v = (im - par[s : s + 1]) * inverse
            total += (0.5 * (1.0 + lax.erf(v))) * par[8 + s : 9 + s]
        loss = value_ref[:, here] * total
        a, b = split2(loss)
        loss_ref[:, here] = jnp.concatenate([a, b], axis=0)
        tract_low = lax.rem(tract_ref[:, here], 128)
        lo_hot[:, here] = jnp.where(
            lax.broadcasted_iota(jnp.int32, (128, width), 0) == tract_low, 1.0, 0.0
        ).astype(BF16)

    onehot_gather(table, local_ref, math.gcd(count, 512), 256, store)

    local_total = jnp.sum(loss_ref[:rr] + loss_ref[rr:], axis=1, keepdims=True)
    local_total = jnp.broadcast_to(local_total, (rr, 128))
    per_dev = TRACT_DEV // 128
    tract_high = tract_ref[...] // 128

    def one_owner(d, carry):
        left = jnp.concatenate(
            [
                jnp.where(tract_high == d * per_dev + h, loss_ref[...], 0.0).astype(BF16)
                for h in range(per_dev)
            ],
            axis=0,
        )
        sums = lax.dot_general(
            left, lo_hot[...], (((1,), (1,)), ((), ())), preferred_element_type=F32
        )
        for h in range(per_dev):
            base = h * 2 * rr
            send[d, :, h * 128 : (h + 1) * 128] = (
                sums[base : base + rr] + sums[base + rr : base + 2 * rr]
            )
        send[d, :, TRACT_DEV:] = local_total
        return carry

    lax.fori_loop(0, n_site, one_owner, 0)
    pl.semaphore_wait(barrier, n_site - 1)

    def copy(j):
        peer = lax.rem(me_s + j, n_site)
        return pltpu.make_async_remote_copy(
            src_ref=send.at[peer],
            dst_ref=recv.at[me_s],
            send_sem=s_sem.at[j],
            recv_sem=r_sem.at[j],
            device_id=(peer, me_r),
            device_id_type=MESH,
        )

    for j in range(1, n_site):
        copy(j).start()
    recv[me_s] = send[me_s]
    for j in range(1, n_site):
        copy(j).wait_recv()
    total = recv[0]
    for s in range(1, n_site):
        total += recv[s]
    out_ref[...] = total[:, :TRACT_DEV]
    sum_ref[...] = total[:, TRACT_DEV:] / all_buildings
    for j in range(1, n_site):
        copy(j).wait_send()


def shards(
    n_site,
    n_real,
    field,
    observed,
    inv_cov,
    site_xy,
    station_site,
    site_mean,
    building_site,
    building_class,
    building_tract,
    building_value,
    median_ln,
    beta_ln,
    loss_step,
):
    rr, sites = field.shape
    ns, cols = inv_cov.shape
    first_site = lax.axis_index("site") * sites
    reals = rr * n_real
    per = n_site // n_real
    tw = 256
    groups = 5
    steps = cols // groups // tw
    nbuf = min(6, groups * steps)
    gw = tw * steps
    rows_o = reals // n_site
    k = 16 // rows_o
    bw = math.gcd(sites, 512)
    kb = max(1, 16 // rr)
    vmem = pl.BlockSpec(memory_space=pltpu.VMEM)
    dma = pltpu.SemaphoreType.DMA
    cond = pl.pallas_call(
        functools.partial(krige_kernel, n_site, n_real, groups, steps, nbuf),
        out_shape=jax.ShapeDtypeStruct((rr, sites), F32),
        in_specs=[vmem, vmem, pl.BlockSpec(memory_space=pl.ANY), vmem, vmem],
        out_specs=vmem,
        scratch_shapes=[
            pltpu.VMEM((2 * rr + 16, sites), BF16),
            pltpu.VMEM((n_real, 2 * rr, ns), BF16),
            pltpu.VMEM((per + 1, 8, ns), F32),
            pltpu.VMEM((cols, 8), F32),
            pltpu.VMEM((nbuf, ns, tw), F32),
            pltpu.VMEM((cols, sites), BF16),
            pltpu.VMEM((groups, n_site, rows_o, gw), F32),
            pltpu.VMEM((groups, n_site, rows_o, gw), F32),
            pltpu.VMEM((groups, n_site, 16, gw // k), BF16),
            pltpu.VMEM((reals, sites), F32),
            pltpu.VMEM((sites // bw, n_real, kb * rr, bw // kb), BF16),
            pltpu.VMEM((sites // bw, n_real, kb * rr, bw // kb), BF16),
            dma((nbuf,)),
            dma((n_real,)),
            dma((n_real,)),
            dma((n_site,)),
            dma((per,)),
            dma((groups, n_site)),
            dma((groups, n_site)),
            dma((groups, n_site)),
            dma((groups, n_site)),
            dma((sites // bw, n_real)),
            dma((sites // bw, n_real)),
        ],
        compiler_params=pltpu.CompilerParams(
            collective_id=0, has_side_effects=True, vmem_limit_bytes=56 * 2**20
        ),
    )(
        field,
        observed.reshape(1, ns),
        inv_cov,
        site_xy,
        (station_site - first_site).reshape(1, ns),
    )
    count = building_site.shape[0]
    classes = median_ln.shape[1]
    params = jnp.concatenate(
        [median_ln, beta_ln[None, :], jnp.ones((3, classes), F32), loss_step, jnp.ones((4, classes), F32)]
    )
    params = jnp.pad(params, ((0, 0), (0, 128 - classes)))
    tract, total = pl.pallas_call(
        functools.partial(loss_kernel, n_site, count * n_site),
        out_shape=(
            jax.ShapeDtypeStruct((rr, TRACT_DEV), F32),
            jax.ShapeDtypeStruct((rr, 128), F32),
        ),
        in_specs=[vmem] * 7,
        out_specs=(vmem, vmem),
        scratch_shapes=[
            pltpu.VMEM((2 * rr, sites), BF16),
            pltpu.VMEM((2 * rr, count), F32),
            pltpu.VMEM((128, count), BF16),
            pltpu.VMEM((n_site, rr, TRACT_DEV + 128), F32),
            pltpu.VMEM((n_site, rr, TRACT_DEV + 128), F32),
            dma((n_site,)),
            dma((n_site,)),
        ],
        compiler_params=pltpu.CompilerParams(
            collective_id=1, has_side_effects=True, vmem_limit_bytes=40 * 2**20
        ),
    )(
        cond,
        site_mean.reshape(1, sites),
        (building_site - first_site).reshape(1, count),
        building_class.reshape(1, count),
        building_tract.reshape(1, count),
        building_value.reshape(1, count),
        params,
    )
    return cond, tract, total[:, 0]


def solution(mesh):
    placed = (
        P("real", "site"),
        P("site"),
        P("site", "real"),
        P(None, "site"),
        P("site"),
        P("site"),
        P("site"),
        P("site"),
        P("site"),
        P("site"),
        P(),
        P(),
        P(),
    )
    return jax.shard_map(
        functools.partial(shards, mesh.shape["site"], mesh.shape["real"]),
        mesh=mesh,
        in_specs=placed,
        out_specs=(P("real", "site"), P("real", "site"), P("real")),
        check_vma=False,
    )
```

```python
import functools
import math

import jax
import jax.numpy as jnp
from jax import lax
from jax.experimental import pallas as pl
from jax.experimental.pallas import tpu as pltpu
from jax.sharding import PartitionSpec as P

MESH = pl.DeviceIdType.MESH
F32 = jnp.float32
BF16 = jnp.bfloat16
COORD_SCALE = math.log2(math.e) / 30.0
TRACT_DEV = 512


def split2(x):
    hi = x.astype(BF16).astype(F32)
    return hi, x - hi


def split3(x):
    hi, rest = split2(x)
    mid, low = split2(rest)
    return hi, mid, low


def onehot_gather(table_ref, index_ref, width, block, store):
    count = index_ref.shape[1]
    sites = table_ref.shape[1]

    def chunk(n, carry):
        start = pl.multiple_of(n * width, 128)
        index = index_ref[:, pl.ds(start, width)]
        total = jnp.zeros((table_ref.shape[0], width), F32)
        for s in range(sites // block):
            rows = lax.broadcasted_iota(jnp.int32, (block, width), 0) + s * block
            hot = jnp.where(rows == index, 1.0, 0.0).astype(BF16)
            total += jnp.dot(
                table_ref[:, s * block : (s + 1) * block], hot, preferred_element_type=F32
            )
        store(start, total)
        return carry

    lax.fori_loop(0, count // width, chunk, 0)


def krige_kernel(
    n_site,
    n_real,
    groups,
    steps,
    nbuf,
    field_ref,
    observed_ref,
    inv_ref,
    xy_ref,
    local_ref,
    cond_ref,
    table,
    innov_all,
    xy_rows,
    xy_col,
    tiles,
    cross,
    part,
    got,
    wout,
    acc,
    back,
    back_in,
    tile_sem,
    i_send,
    i_recv,
    x_send,
    x_recv,
    p_send,
    p_recv,
    w_send,
    w_recv,
    b_send,
    b_recv,
):
    me_s = lax.axis_index("site")
    me_r = lax.axis_index("real")
    rr, sites = field_ref.shape
    ns = observed_ref.shape[1]
    reals = n_real * rr
    per = n_site // n_real
    tw = tiles.shape[2]
    gw = tw * steps
    rows_o = reals // n_site
    k = 16 // rows_o
    mw = gw // k
    total_steps = groups * steps
    cols_all = total_steps * tw

    barrier = pltpu.get_barrier_semaphore()
    for j in range(1, n_site):
        pl.semaphore_signal(
            barrier, inc=1, device_id=(lax.rem(me_s + j, n_site), me_r), device_id_type=MESH
        )
    for j in range(1, n_real):
        pl.semaphore_signal(
            barrier, inc=1, device_id=(me_s, lax.rem(me_r + j, n_real)), device_id_type=MESH
        )

    def tile_copy(c):
        slot = lax.rem(c, nbuf)
        col = pl.multiple_of(c * tw, 128)
        return pltpu.make_async_copy(
            inv_ref.at[:, pl.ds(col, tw)], tiles.at[slot], tile_sem.at[slot]
        )

    for c in range(nbuf):
        tile_copy(c).start()

    fh, fl = split2(field_ref[...])
    xa, xb, xc = split3(xy_ref[...] * COORD_SCALE)
    table[...] = jnp.concatenate(
        [fh, fl, xa, xb, xc, jnp.zeros((10, sites), F32)], axis=0
    ).astype(BF16)

    me_slot = lax.rem(me_s, per)
    mine = me_s // per == me_r

    def store(start, got_rows):
        width = got_rows.shape[1]
        station = got_rows[:rr] + got_rows[rr : 2 * rr]
        xys = (
            got_rows[2 * rr : 2 * rr + 2]
            + got_rows[2 * rr + 2 : 2 * rr + 4]
            + got_rows[2 * rr + 4 : 2 * rr + 6]
        )
        innov = observed_ref[:, pl.ds(start, width)] - station
        hi, low = split2(innov)
        innov_all[me_r, :, pl.ds(start, width)] = jnp.concatenate([hi, low], axis=0).astype(BF16)
        xy_rows[per, :, pl.ds(start, width)] = jnp.concatenate(
            [xys, jnp.zeros((6, width), F32)], axis=0
        )

    onehot_gather(table, local_ref, math.gcd(ns, 512), 256, store)

    pl.semaphore_wait(barrier, n_site - 1 + n_real - 1)

    def innov_copy(j):
        return pltpu.make_async_remote_copy(
            src_ref=innov_all.at[me_r],
            dst_ref=innov_all.at[me_r],
            send_sem=i_send.at[j],
            recv_sem=i_recv.at[j],
            device_id=(me_s, lax.rem(me_r + j, n_real)),
            device_id_type=MESH,
        )

    def xy_copy(j):
        return pltpu.make_async_remote_copy(
            src_ref=xy_rows.at[per],
            dst_ref=xy_rows.at[me_slot],
            send_sem=x_send.at[j],
            recv_sem=x_recv.at[me_slot],
            device_id=(lax.rem(me_s + j, n_site), me_r),
            device_id_type=MESH,
        )

    @pl.when(mine)
    def _():
        for j in range(1, n_site):
            xy_copy(j).start()

    for j in range(1, n_real):
        innov_copy(j).start()

    @pl.when(mine)
    def _():
        xy_rows[me_slot] = xy_rows[per]

    for s in range(per):

        @pl.when(jnp.logical_not(jnp.logical_and(mine, me_slot == s)))
        def _():
            pltpu.make_async_remote_copy(
                src_ref=xy_rows.at[per],
                dst_ref=xy_rows.at[s],
                send_sem=x_send.at[0],
                recv_sem=x_recv.at[s],
                device_id=(lax.rem(me_s + 1, n_site), me_r),
                device_id_type=MESH,
            ).wait_recv()

    for s in range(per):
        xy_col[s * ns : (s + 1) * ns, :] = xy_rows[s].T

    east = xy_ref[0:1, :] * COORD_SCALE
    north = xy_ref[1:2, :] * COORD_SCALE
    kt = math.gcd(ns, 256)
    k_count = ns // kt
    pieces = tw // 32
    early = cols_all // 2

    def cross_piece(row):
        row = pl.multiple_of(row, 16)
        dx = xy_col[pl.ds(row, 16), 0:1] - east
        dy = xy_col[pl.ds(row, 16), 1:2] - north
        d2 = jnp.maximum(dx * dx + dy * dy, 1e-20)
        cross[pl.ds(row, 16), :] = jnp.exp2(-(d2 * lax.rsqrt(d2))).astype(BF16)

    def early_pieces(n, carry):
        for m in range(8):
            cross_piece(n * 128 + m * 16)
        return carry

    lax.fori_loop(0, early // 128, early_pieces, 0)
    acc[...] = jnp.zeros_like(acc)
    for j in range(1, n_real):
        innov_copy(j).wait_recv()

    def part_copy(g, j):
        peer = lax.rem(me_s + j, n_site)
        return pltpu.make_async_remote_copy(
            src_ref=part.at[g, peer],
            dst_ref=got.at[g, me_s],
            send_sem=p_send.at[g, j],
            recv_sem=p_recv.at[g, j],
            device_id=(peer, me_r),
            device_id_type=MESH,
        )

    def w_copy(g, j):
        peer = lax.rem(me_s + j, n_site)
        return pltpu.make_async_remote_copy(
            src_ref=wout.at[g, me_s],
            dst_ref=wout.at[g, me_s],
            send_sem=w_send.at[g, j],
            recv_sem=w_recv.at[g, j],
            device_id=(peer, me_r),
            device_id_type=MESH,
        )

    def sum_and_share(g):
        for j in range(1, n_site):
            part_copy(g, j).wait_recv()
        got[g, me_s] = part[g, me_s]
        total = got[g, 0]
        for s in range(1, n_site):
            total += got[g, s]
        wout[g, me_s] = jnp.concatenate(
            [total[:, i * mw : (i + 1) * mw] for i in range(k)], axis=0
        ).astype(BF16)
        for j in range(1, n_site):
            w_copy(g, j).start()

    def apply_group(g, width, after):
        for j in range(1, n_site):
            w_copy(g, j).wait_recv()
        weights = wout[g].astype(F32)
        weights = jnp.concatenate(
            [
                jnp.concatenate(
                    [weights[s, i * rows_o : (i + 1) * rows_o] for i in range(k)], axis=1
                )
                for s in range(n_site)
            ],
            axis=0,
        ).astype(BF16)
        row = pl.multiple_of(g * gw, 128)
        for n in range(sites // width):
            cols = slice(n * width, (n + 1) * width)
            acc[:, cols] += jnp.dot(
                weights, cross[pl.ds(row, gw), cols], preferred_element_type=F32
            )
            after(n)

    def one_step(q, g):
        c = g * steps + q
        slot = lax.rem(c, nbuf)
        tile_copy(c).wait()
        lhs = innov_all[...].reshape(n_real * 2 * rr, ns)
        product = jnp.zeros((n_real * 2 * rr, tw), F32)
        done = 0
        for p in range(k_count):
            product += jnp.dot(
                lhs[:, p * kt : (p + 1) * kt],
                tiles[slot, p * kt : (p + 1) * kt, :].astype(BF16),
                preferred_element_type=F32,
            )
            upto = (p + 1) * pieces // k_count
            for m in range(done, upto):
                cross_piece(early + c * (tw // 2) + m * 16)
            done = upto
        product = product.reshape(n_real, 2, rr, tw)
        partial = (product[:, 0] + product[:, 1]).reshape(n_site, rows_o, tw)
        part[g, :, :, pl.ds(pl.multiple_of(q * tw, 128), tw)] = partial

        @pl.when(c + nbuf < total_steps)
        def _():
            tile_copy(c + nbuf).start()

        return g

    def one_group(g, carry):
        lax.fori_loop(0, steps, one_step, g)
        for j in range(1, n_site):
            part_copy(g, j).start()

        @pl.when(g >= 1)
        def _():
            sum_and_share(g - 1)

        @pl.when(g >= 2)
        def _():
            apply_group(g - 2, 512, lambda n: None)

        return carry

    lax.fori_loop(0, groups, one_group, 0)

    def back_copy(j, n):
        peer = lax.rem(me_r + j, n_real)
        return pltpu.make_async_remote_copy(
            src_ref=back.at[n, peer],
            dst_ref=back_in.at[n, me_r],
            send_sem=b_send.at[n, j],
            recv_sem=b_recv.at[n, j],
            device_id=(me_s, peer),
            device_id_type=MESH,
        )

    bw = back.shape[3] * (back.shape[2] // rr)
    kb = bw // back.shape[3]

    def send_back(n):
        for z in range(n_real):
            block = acc[z * rr : (z + 1) * rr, n * bw : (n + 1) * bw]
            w = bw // kb
            back[n, z] = jnp.concatenate(
                [block[:, i * w : (i + 1) * w] for i in range(kb)], axis=0
            ).astype(BF16)
        for j in range(1, n_real):
            back_copy(j, n).start()

    sum_and_share(groups - 1)
    apply_group(groups - 2, 512, lambda n: None)
    apply_group(groups - 1, bw, send_back)

    own_row = pl.multiple_of(me_r * rr, 8)
    for n in range(sites // bw):
        for j in range(1, n_real):
            back_copy(j, n).wait_recv()
        back_in[n, me_r] = jnp.zeros_like(back_in[n, 0])
        total = back_in[n, 0].astype(F32)
        for z in range(1, n_real):
            total += back_in[n, z].astype(F32)
        total = jnp.concatenate([total[i * rr : (i + 1) * rr] for i in range(kb)], axis=1)
        cols = slice(n * bw, (n + 1) * bw)
        cond_ref[:, cols] = field_ref[:, cols] + acc[pl.ds(own_row, rr), cols] + total

    for j in range(1, n_real):
        innov_copy(j).wait_send()
        for n in range(sites // bw):
            back_copy(j, n).wait_send()

    @pl.when(mine)
    def _():
        for j in range(1, n_site):
            xy_copy(j).wait_send()

    def drain(g, carry):
        for j in range(1, n_site):
            part_copy(g, j).wait_send()
            w_copy(g, j).wait_send()
        return carry

    lax.fori_loop(0, groups, drain, 0)


def loss_kernel(
    n_site,
    all_buildings,
    cond_ref,
    mean_ref,
    local_ref,
    class_ref,
    tract_ref,
    value_ref,
    params_ref,
    out_ref,
    sum_ref,
    table,
    loss_ref,
    lo_hot,
    send,
    recv,
    s_sem,
    r_sem,
):
    me_s = lax.axis_index("site")
    me_r = lax.axis_index("real")
    rr = cond_ref.shape[0]
    count = local_ref.shape[1]
    barrier = pltpu.get_barrier_semaphore()
    for j in range(1, n_site):
        pl.semaphore_signal(
            barrier, inc=1, device_id=(lax.rem(me_s + j, n_site), me_r), device_id_type=MESH
        )
    hi, low = split2(mean_ref[...] + 0.6 * cond_ref[...])
    table[...] = jnp.concatenate([hi, low], axis=0).astype(BF16)
    classes = params_ref.shape[1]

    def store(start, rows):
        width = rows.shape[1]
        here = pl.ds(start, width)
        im = rows[:rr] + rows[rr:]
        hot = jnp.where(
            lax.broadcasted_iota(jnp.int32, (classes, width), 0) == class_ref[:, here], 1.0, 0.0
        )
        par = jnp.dot(
            params_ref[...], hot, precision=lax.Precision.HIGHEST, preferred_element_type=F32
        )
        inverse = 0.7071067811865476 / par[4:5]
        total = jnp.zeros((rr, width), F32)
        for s in range(4):
            v = (im - par[s : s + 1]) * inverse
            total += (0.5 * (1.0 + lax.erf(v))) * par[8 + s : 9 + s]
        loss = value_ref[:, here] * total
        a, b = split2(loss)
        loss_ref[:, here] = jnp.concatenate([a, b], axis=0)
        tract_low = lax.rem(tract_ref[:, here], 128)
        lo_hot[:, here] = jnp.where(
            lax.broadcasted_iota(jnp.int32, (128, width), 0) == tract_low, 1.0, 0.0
        ).astype(BF16)

    onehot_gather(table, local_ref, math.gcd(count, 512), 256, store)

    local_total = jnp.sum(loss_ref[:rr] + loss_ref[rr:], axis=1, keepdims=True)
    local_total = jnp.broadcast_to(local_total, (rr, 128))
    per_dev = TRACT_DEV // 128
    tract_high = tract_ref[...] // 128

    def one_owner(d, carry):
        left = jnp.concatenate(
            [
                jnp.where(tract_high == d * per_dev + h, loss_ref[...], 0.0).astype(BF16)
                for h in range(per_dev)
            ],
            axis=0,
        )
        sums = lax.dot_general(
            left, lo_hot[...], (((1,), (1,)), ((), ())), preferred_element_type=F32
        )
        for h in range(per_dev):
            base = h * 2 * rr
            send[d, :, h * 128 : (h + 1) * 128] = (
                sums[base : base + rr] + sums[base + rr : base + 2 * rr]
            )
        send[d, :, TRACT_DEV:] = local_total
        return carry

    lax.fori_loop(0, n_site, one_owner, 0)
    pl.semaphore_wait(barrier, n_site - 1)

    def copy(j):
        peer = lax.rem(me_s + j, n_site)
        return pltpu.make_async_remote_copy(
            src_ref=send.at[peer],
            dst_ref=recv.at[me_s],
            send_sem=s_sem.at[j],
            recv_sem=r_sem.at[j],
            device_id=(peer, me_r),
            device_id_type=MESH,
        )

    for j in range(1, n_site):
        copy(j).start()
    recv[me_s] = send[me_s]
    for j in range(1, n_site):
        copy(j).wait_recv()
    total = recv[0]
    for s in range(1, n_site):
        total += recv[s]
    out_ref[...] = total[:, :TRACT_DEV]
    sum_ref[...] = total[:, TRACT_DEV:] / all_buildings
    for j in range(1, n_site):
        copy(j).wait_send()


def shards(
    n_site,
    n_real,
    field,
    observed,
    inv_cov,
    site_xy,
    station_site,
    site_mean,
    building_site,
    building_class,
    building_tract,
    building_value,
    median_ln,
    beta_ln,
    loss_step,
):
    rr, sites = field.shape
    ns, cols = inv_cov.shape
    first_site = lax.axis_index("site") * sites
    reals = rr * n_real
    per = n_site // n_real
    tw = 256
    groups = 4
    steps = cols // groups // tw
    nbuf = min(6, groups * steps)
    gw = tw * steps
    rows_o = reals // n_site
    k = 16 // rows_o
    bw = math.gcd(sites, 512)
    kb = max(1, 16 // rr)
    vmem = pl.BlockSpec(memory_space=pltpu.VMEM)
    dma = pltpu.SemaphoreType.DMA
    cond = pl.pallas_call(
        functools.partial(krige_kernel, n_site, n_real, groups, steps, nbuf),
        out_shape=jax.ShapeDtypeStruct((rr, sites), F32),
        in_specs=[vmem, vmem, pl.BlockSpec(memory_space=pl.ANY), vmem, vmem],
        out_specs=vmem,
        scratch_shapes=[
            pltpu.VMEM((2 * rr + 16, sites), BF16),
            pltpu.VMEM((n_real, 2 * rr, ns), BF16),
            pltpu.VMEM((per + 1, 8, ns), F32),
            pltpu.VMEM((cols, 8), F32),
            pltpu.VMEM((nbuf, ns, tw), F32),
            pltpu.VMEM((cols, sites), BF16),
            pltpu.VMEM((groups, n_site, rows_o, gw), F32),
            pltpu.VMEM((groups, n_site, rows_o, gw), F32),
            pltpu.VMEM((groups, n_site, 16, gw // k), BF16),
            pltpu.VMEM((reals, sites), F32),
            pltpu.VMEM((sites // bw, n_real, kb * rr, bw // kb), BF16),
            pltpu.VMEM((sites // bw, n_real, kb * rr, bw // kb), BF16),
            dma((nbuf,)),
            dma((n_real,)),
            dma((n_real,)),
            dma((n_site,)),
            dma((per,)),
            dma((groups, n_site)),
            dma((groups, n_site)),
            dma((groups, n_site)),
            dma((groups, n_site)),
            dma((sites // bw, n_real)),
            dma((sites // bw, n_real)),
        ],
        compiler_params=pltpu.CompilerParams(
            collective_id=0, has_side_effects=True, vmem_limit_bytes=56 * 2**20
        ),
    )(
        field,
        observed.reshape(1, ns),
        inv_cov,
        site_xy,
        (station_site - first_site).reshape(1, ns),
    )
    count = building_site.shape[0]
    classes = median_ln.shape[1]
    params = jnp.concatenate(
        [median_ln, beta_ln[None, :], jnp.ones((3, classes), F32), loss_step, jnp.ones((4, classes), F32)]
    )
    params = jnp.pad(params, ((0, 0), (0, 128 - classes)))
    tract, total = pl.pallas_call(
        functools.partial(loss_kernel, n_site, count * n_site),
        out_shape=(
            jax.ShapeDtypeStruct((rr, TRACT_DEV), F32),
            jax.ShapeDtypeStruct((rr, 128), F32),
        ),
        in_specs=[vmem] * 7,
        out_specs=(vmem, vmem),
        scratch_shapes=[
            pltpu.VMEM((2 * rr, sites), BF16),
            pltpu.VMEM((2 * rr, count), F32),
            pltpu.VMEM((128, count), BF16),
            pltpu.VMEM((n_site, rr, TRACT_DEV + 128), F32),
            pltpu.VMEM((n_site, rr, TRACT_DEV + 128), F32),
            dma((n_site,)),
            dma((n_site,)),
        ],
        compiler_params=pltpu.CompilerParams(
            collective_id=1, has_side_effects=True, vmem_limit_bytes=40 * 2**20
        ),
    )(
        cond,
        site_mean.reshape(1, sites),
        (building_site - first_site).reshape(1, count),
        building_class.reshape(1, count),
        building_tract.reshape(1, count),
        building_value.reshape(1, count),
        params,
    )
    return cond, tract, total[:, 0]


def solution(mesh):
    placed = (
        P("real", "site"),
        P("site"),
        P("site", "real"),
        P(None, "site"),
        P("site"),
        P("site"),
        P("site"),
        P("site"),
        P("site"),
        P("site"),
        P(),
        P(),
        P(),
    )
    return jax.shard_map(
        functools.partial(shards, mesh.shape["site"], mesh.shape["real"]),
        mesh=mesh,
        in_specs=placed,
        out_specs=(P("real", "site"), P("real", "site"), P("real")),
        check_vma=False,
    )
```
